512 devices in a mesh: pipe: 16 (over y, core), expert: 32 (over x, z).
Axes of the slice: x: 4, y: 8, z: 8, core: 2. Of those that a mesh axis runs over, the one named last changes fastest.
Arguments:
- x_forward: bfloat16 [16, 2048, 3584], P('pipe', 'expert'), may hold values from -6 to 6
- x_backward: bfloat16 [16, 2048, 3584], P('pipe', 'expert'), may hold values from -6 to 6
- norm_gain: float32 [16, 3584], P('pipe'), may hold values from 0.1 to 1.9
- w_gate: bfloat16 [16, 3584, 4096], P('pipe', None, 'expert'), may hold values from -0.09375 to 0.09375
- w_up: bfloat16 [16, 3584, 4096], P('pipe', None, 'expert'), may hold values from -0.09375 to 0.09375
- w_down: bfloat16 [16, 4096, 3584], P('pipe', 'expert'), may hold values from -0.1875 to 0.1875
- routes_forward: int32 [16, 2048, 1], P('pipe', 'expert'), may hold values from 0 to 3; in each aligned block of 64 rows (0 to 63, 64 to 127, ..., all dimensions but the last counted through in order) at most 16 rows name the same one
- routes_backward: int32 [16, 2048, 1], P('pipe', 'expert'), may hold values from 0 to 3; in each aligned block of 64 rows (0 to 63, 64 to 127, ..., all dimensions but the last counted through in order) at most 16 rows name the same one
- gates_forward: float32 [16, 2048, 1], P('pipe', 'expert'), may hold values from 0.2 to 2
- gates_backward: float32 [16, 2048, 1], P('pipe', 'expert'), may hold values from 0.2 to 2
Outputs:
- out_forward: bfloat16 [16, 2048, 3584], P('pipe', 'expert')
- out_backward: bfloat16 [16, 2048, 3584], P('pipe', 'expert')
The draws below stay inside these ranges and needn't reach their ends.
Inputs may be any that keep to these rules, and one draw needn't show every extreme that they name: `routes_forward`: each row names one expert; in each aligned block of 64 rows (the rows of one device) every expert is named by exactly 16 rows. `routes_backward`: as for routes_forward.
All inputs are finite; a program needn't handle non-finite values.
Results may differ from the reference program's by a relative error of at most 0.0085.
Values may be sent and summed in bfloat16 or wider, within the bound.
No kernel may reach another device: no remote copies, remote signals or barrier semaphores. Data moves between devices by JAX's collectives and lax.ppermute only.
A program may use at most 64 MiB of HBM per device.

```python
import math
import jax
import jax.numpy as jnp
import numpy as np
from jax import lax

D = 3584
FFW = 1024
EXPERTS = 4
TOP = 1
TOK_DEV = 64
SECTIONS = 16
CAP_MB = 16
TOKENS = 2048
N_EXPERT = 32


def block_levels(rng, dims, cuts, low, largest):
    gain, own = 1.0, jax.random.fold_in(rng, 6)
    for axis_at, shards_of in cuts:
        steps = jnp.exp(jax.random.uniform(jax.random.fold_in(own, axis_at), (shards_of,), jnp.float32, low / len(cuts), largest / len(cuts)))
        gain = gain * jnp.repeat(steps, dims[axis_at] // shards_of).reshape([-1 if axis == axis_at else 1 for axis in range(len(dims))])
    return gain


def routed_block(rng, own, number, rows, count, top, limit, lean):
    order = jax.random.permutation(rng, count)
    crowded, ordinary = portions_of(count, rows * top, limit, lean, True), portions_of(count, rows * top, limit, lean, False)
    places = jnp.arange(count)

    def named(lengths, turn):
        used = int((lengths > 0).sum())
        fixed = max(1, used // 4)
        shifted = fixed + (places - fixed + turn * (used - fixed)) % max(1, count - fixed)
        return jnp.zeros((count,), jnp.int32).at[order[jnp.where(places < fixed, places, shifted)]].set(jnp.asarray(lengths, jnp.int32))

    lengths = jnp.where(number % 4 == 0, named(crowded, number // 4), named(ordinary, number - number // 4 - 1))
    mixed = jax.random.permutation(jax.random.fold_in(own, 3), count)
    source_of, receiver = mixed[0:count // 2 * 2:2], mixed[1:count // 2 * 2:2]
    margin = jnp.minimum(lengths[source_of] - 1, limit - lengths[receiver]) // 2
    margin = jnp.where((source_of == order[0]) | (receiver == order[0]) | (lengths[receiver] == 0), 0, jnp.maximum(margin, 0))
    shifted = jax.random.randint(jax.random.fold_in(own, 4), (count // 2,), 0, 1 << 20) % (margin + 1)
    lengths = lengths.at[source_of].add(-shifted).at[receiver].add(shifted)
    items = jnp.searchsorted(jnp.cumsum(lengths), jnp.arange(rows * top), side="right").astype(jnp.int32)
    table = items.reshape(top, rows).T
    table = table[jax.random.permutation(jax.random.fold_in(own, 1), rows)]
    turn = jax.random.randint(jax.random.fold_in(own, 2), (rows, 1), 0, top)
    return jnp.take_along_axis(table, (jnp.arange(top)[None, :] + turn) % top, axis=1)


def portions_of(number_of, total, bound, slope, full):
    weights = [(1 << 20) // math.isqrt(standing ** slope) + 1 for standing in range(1, number_of + 1)]
    largest = bound if full else min(bound, max(-(-total // number_of), total * weights[0] // sum(weights)))
    least = 1 if total - largest >= number_of - 1 else 0
    given, spare = [largest] + [least] * (number_of - 1), total - largest - least * (number_of - 1)
    while spare > 0:
        free = [i for i in range(1, number_of) if given[i] < largest] or [i for i in range(1, number_of) if given[i] < bound]
        mass, left = sum([weights[i] for i in free]), spare
        for i in free:
            more = min(bound - given[i], max(1, left * weights[i] // mass), spare)
            given[i] = given[i] + more
            spare = spare - more
    return np.array(given)


def normal_values(stream_key, extent, width, limit, cuts=(), dtype=jnp.bfloat16):
    loudness = block_levels(stream_key, extent, cuts, -0.22, 0.18) if cuts else 1.0
    array = jax.random.normal(stream_key, extent, jnp.float32) * width * loudness
    return jnp.minimum(jnp.maximum(array, -limit), limit).astype(dtype)


def setup_inputs(seed: int = 0) -> dict:
    seeds = jax.random.split(jax.random.key(seed), 11)
    x_forward = normal_values(seeds[0], (SECTIONS, TOKENS, D), 1.0, 6.0, ((0, 16), (1, 32)))
    x_backward = normal_values(seeds[1], (SECTIONS, TOKENS, D), 1.0, 6.0, ((0, 16), (1, 32)))
    norm_gain = jnp.clip(1.0 + 0.18 * jax.random.normal(seeds[2], (SECTIONS, D), jnp.float32), 0.1, 1.9)
    w_gate = normal_values(seeds[3], (SECTIONS, D, EXPERTS * FFW), D ** -0.5, 0.09375, ((0, 16), (2, 32)))
    w_up = normal_values(seeds[4], (SECTIONS, D, EXPERTS * FFW), D ** -0.5, 0.09375, ((0, 16), (2, 32)))
    w_down = normal_values(seeds[5], (SECTIONS, EXPERTS * FFW, D), FFW ** -0.5, 0.1875, ((0, 16), (1, 32)))
    routes_forward_keys = jax.random.split(jax.random.fold_in(seeds[6], 1), SECTIONS * TOKENS // TOK_DEV)
    routes_forward_turns = jax.random.permutation(jax.random.fold_in(seeds[6], 3), SECTIONS * TOKENS // TOK_DEV)
    routes_forward = jax.vmap(lambda own, number: routed_block(jax.random.fold_in(seeds[6], 2), own, number, TOK_DEV, EXPERTS, TOP, CAP_MB, 0))(routes_forward_keys, routes_forward_turns).reshape((SECTIONS, TOKENS, TOP))
    routes_backward_keys = jax.random.split(jax.random.fold_in(seeds[7], 1), SECTIONS * TOKENS // TOK_DEV)
    routes_backward_turns = jax.random.permutation(jax.random.fold_in(seeds[7], 3), SECTIONS * TOKENS // TOK_DEV)
    routes_backward = jax.vmap(lambda own, number: routed_block(jax.random.fold_in(seeds[7], 2), own, number, TOK_DEV, EXPERTS, TOP, CAP_MB, 0))(routes_backward_keys, routes_backward_turns).reshape((SECTIONS, TOKENS, TOP))
    gates_forward = jnp.clip(jnp.exp(math.log(2.0) - 2.3025851 * jax.random.uniform(seeds[8], (SECTIONS, TOKENS, TOP), jnp.float32) ** block_levels(seeds[8], (SECTIONS, TOKENS, TOP), ((0, 16), (1, 32)), -0.2, 0.2)), 0.2, 2.0)
    gates_backward = jnp.clip(jnp.exp(math.log(2.0) - 2.3025851 * jax.random.uniform(seeds[9], (SECTIONS, TOKENS, TOP), jnp.float32) ** block_levels(seeds[9], (SECTIONS, TOKENS, TOP), ((0, 16), (1, 32)), -0.2, 0.2)), 0.2, 2.0)
    return {"x_forward": x_forward, "x_backward": x_backward, "norm_gain": norm_gain, "w_gate": w_gate, "w_up": w_up, "w_down": w_down, "routes_forward": routes_forward, "routes_backward": routes_backward, "gates_forward": gates_forward, "gates_backward": gates_backward}


def rms_norm(values, norm_scale):
    widened = values.astype(jnp.float32)
    mean_square = lax.optimization_barrier(jnp.mean(widened * widened, axis=-1, keepdims=True))
    return (widened * lax.rsqrt(mean_square + 1e-06) * norm_scale).astype(jnp.bfloat16)

def expert_block(chosen_rows, gate_cols, up_cols, down_rows):
    gate_part = jnp.dot(chosen_rows, gate_cols, preferred_element_type=jnp.float32)
    up_part = jnp.dot(chosen_rows, up_cols, preferred_element_type=jnp.float32)
    hidden = (jax.nn.silu(gate_part) * up_part).astype(jnp.bfloat16)
    shards = N_EXPERT // EXPERTS
    group_width = FFW // shards
    row_count = hidden.shape[0]
    pieces = hidden.astype(jnp.float32).reshape(row_count, shards, group_width)
    down_groups = down_rows.astype(jnp.float32).reshape(shards, group_width, D)
    partial_value = jnp.einsum('rsh,shd->srd', pieces, down_groups).astype(jnp.bfloat16)
    return lax.optimization_barrier(jnp.sum(partial_value.astype(jnp.float32), axis=0))

def moe_layer(states, norm_scale, gate_all, up_all, down_all, routes, gate_vals):
    normed = rms_norm(states, norm_scale)
    combined = jnp.zeros(states.shape, jnp.float32)
    row_count = N_EXPERT * CAP_MB
    for expert_id in range(EXPERTS):
        hit_mask = routes == expert_id
        chosen = jnp.any(hit_mask, axis=1)
        indices = jnp.nonzero(chosen, size=row_count, fill_value=0)[0].astype(jnp.int32)
        low_col = expert_id * FFW
        outputs = expert_block(normed[indices], gate_all[:, low_col:low_col + FFW], up_all[:, low_col:low_col + FFW], down_all[low_col:low_col + FFW])
        weight = lax.optimization_barrier(jnp.sum(jnp.where(hit_mask, gate_vals, jnp.zeros_like(gate_vals)), axis=1))
        combined = combined.at[indices].add(weight[indices][:, None] * outputs)
    return (states.astype(jnp.float32) + combined).astype(jnp.bfloat16)

def reference(x_forward, x_backward, norm_gain, w_gate, w_up, w_down, routes_forward, routes_backward, gates_forward, gates_backward):
    fwd_list = []
    bwd_list = []
    for section_index in range(SECTIONS):
        fwd_list.append(moe_layer(x_forward[section_index], norm_gain[section_index], w_gate[section_index], w_up[section_index], w_down[section_index], routes_forward[section_index], gates_forward[section_index]))
        bwd_list.append(moe_layer(x_backward[section_index], norm_gain[section_index], w_gate[section_index], w_up[section_index], w_down[section_index], routes_backward[section_index], gates_backward[section_index]))
    done_fwd = jnp.stack(fwd_list)
    done_bwd = jnp.stack(bwd_list)
    return (jnp.roll(done_fwd, 1, axis=0), jnp.roll(done_bwd, -1, axis=0))
```

```python
import jax
import jax.numpy as jnp
from jax import lax
from jax.experimental import pallas as pl
from jax.experimental.pallas import tpu as pltpu
from jax.sharding import Mesh, PartitionSpec as P

EXPERTS = 4
EXTRA = 16
VMEM_BYTES = 48 * 1024 * 1024


def vmem_spec():
    return pl.BlockSpec(memory_space=pltpu.VMEM)


def smem_spec():
    return pl.BlockSpec(memory_space=pltpu.SMEM)


def call(kernel, out_shape, arguments, scalars=0, flops=0, moved=0, after=()):
    specs = [smem_spec()] * scalars + [vmem_spec()] * (len(arguments) - scalars)
    specs += [pl.BlockSpec(memory_space=pl.ANY)] * len(after)
    used = len(arguments)

    def ordered(*refs):
        kernel(*refs[:used], *refs[used + len(after) :])

    return pl.pallas_call(
        ordered,
        out_shape=out_shape,
        in_specs=specs,
        out_specs=jax.tree.map(lambda _: vmem_spec(), out_shape),
        compiler_params=pltpu.CompilerParams(vmem_limit_bytes=VMEM_BYTES),
        cost_estimate=pl.CostEstimate(flops=flops, bytes_accessed=moved, transcendentals=0),
    )(*arguments, *after)


def shifted(array, axis, by):
    peers = lax.axis_size(axis)
    return lax.ppermute(array, axis, [(i, (i + by) % peers) for i in range(peers)])


def as_column(row):
    count = row.shape[1]
    place = lax.broadcasted_iota(jnp.int32, (count, count), 0)
    other = lax.broadcasted_iota(jnp.int32, (count, count), 1)
    return jnp.sum(jnp.where(place == other, row, jnp.zeros_like(row)), axis=1, keepdims=True)


def slots(routes, blocks, per_block):
    count = routes.shape[1]
    place = lax.broadcasted_iota(jnp.int32, (count, count), 0)
    other = lax.broadcasted_iota(jnp.int32, (count, count), 1)
    earlier = (as_column(routes) == routes) & (place < other)
    rank = jnp.sum(earlier.astype(jnp.int32), axis=0, keepdims=True)
    return place == blocks * per_block + rank


def prepare_kernel(states, routes, gates, gain, buffer, travelling):
    count = states.shape[0]
    values = states[...].astype(jnp.float32)
    mean_square = jnp.mean(values * values, axis=-1, keepdims=True)
    normed = (values * lax.rsqrt(mean_square + 1e-06) * gain[...]).astype(jnp.bfloat16)
    placing = slots(routes[...], routes[...], count // EXPERTS).astype(jnp.bfloat16)
    buffer[...] = jnp.dot(placing, normed, preferred_element_type=jnp.float32).astype(jnp.bfloat16)
    travelling[:count, :] = states[...]
    extra = travelling.shape[0] - count
    travelling[count:, :] = jnp.zeros((extra, states.shape[1]), jnp.bfloat16)
    gate = gates[...]
    high = gate.astype(jnp.bfloat16).astype(jnp.float32)
    middle = (gate - high).astype(jnp.bfloat16).astype(jnp.float32)
    low = gate - high - middle
    row = lax.broadcasted_iota(jnp.int32, (extra, count), 0)
    table = jnp.zeros((extra, count), jnp.float32)
    for place, term in enumerate((routes[...].astype(jnp.float32), high, middle, low)):
        table = jnp.where(row == place, term, table)
    travelling[count:, :count] = table.astype(jnp.bfloat16)


def prepare(states, routes, gates, gain):
    rows, width = states.shape
    return call(
        prepare_kernel,
        (
            jax.ShapeDtypeStruct((rows, width), jnp.bfloat16),
            jax.ShapeDtypeStruct((rows + EXTRA, width), jnp.bfloat16),
        ),
        (states, routes, gates, gain),
        flops=2 * rows * states.size,
        moved=6 * states.size,
    )


def expert_kernel(blocks, gate_ref, up_ref, down_ref, *outs):
    width = gate_ref.shape[1]
    depth = gate_ref.shape[0]
    step = depth // 7
    rows = [ref[...] for ref in blocks]
    rows = rows[0] if len(rows) == 1 else jnp.concatenate(rows, axis=0)
    total = jnp.zeros((rows.shape[0], 2 * width), jnp.float32)
    for k in range(0, depth, step):
        both = jnp.concatenate([gate_ref[k : k + step, :], up_ref[k : k + step, :]], axis=1)
        total += jnp.dot(rows[:, k : k + step], both, preferred_element_type=jnp.float32)
    gate_part, up_part = total[:, :width], total[:, width:]
    hidden = (gate_part * jax.nn.sigmoid(gate_part) * up_part).astype(jnp.bfloat16)
    for k in range(0, depth, step):
        part = jnp.dot(hidden, down_ref[:, k : k + step], preferred_element_type=jnp.float32)
        part = part.astype(jnp.bfloat16)
        first = 0
        for out in outs:
            count = out.shape[0]
            out[:, k : k + step] = part[first : first + count]
            first += count


def experts(blocks, gate_cols, up_cols, down_rows, after=()):
    number = len(blocks)

    def kernel(*refs):
        expert_kernel(refs[:number], *refs[number:])

    row_count = sum(block.shape[0] for block in blocks)
    return call(
        kernel,
        tuple(jax.ShapeDtypeStruct(block.shape, jnp.bfloat16) for block in blocks),
        (*blocks, gate_cols, up_cols, down_rows),
        flops=6 * row_count * gate_cols.size,
        moved=6 * gate_cols.size + 4 * sum(block.size for block in blocks),
        after=after,
    )


def add(parts, sums, after):
    number = len(parts)

    def kernel(*refs):
        for part, received, out in zip(refs[:number], refs[number:], refs[2 * number :]):
            total = part[...].astype(jnp.float32) + received[...].astype(jnp.float32)
            out[...] = total.astype(jnp.bfloat16)

    return call(
        kernel,
        tuple(jax.ShapeDtypeStruct(part.shape, jnp.bfloat16) for part in parts),
        (*parts, *sums),
        flops=sum(part.size for part in parts),
        moved=6 * sum(part.size for part in parts),
        after=after,
    )


def split_kernel(x_ref, own, from_left, from_right, *outs):
    count = outs[0].shape[0]
    for d, out in enumerate(outs):
        start = pl.multiple_of(lax.rem(x_ref[0] + d, EXPERTS) * count, count)
        rows = pl.ds(start, count)
        total = own[rows, :].astype(jnp.float32) + from_left[rows, :].astype(jnp.float32)
        out[...] = (total + from_right[rows, :].astype(jnp.float32)).astype(jnp.bfloat16)


def split(x_index, own, from_left, from_right):
    rows, width = own.shape
    return call(
        split_kernel,
        tuple(jax.ShapeDtypeStruct((rows // EXPERTS, width), jnp.bfloat16) for _ in range(EXPERTS)),
        (x_index, own, from_left, from_right),
        scalars=1,
        flops=2 * own.size,
        moved=8 * own.size,
    )


def combine_kernel(x_ref, travelled, *refs):
    blocks, out = refs[:-1], refs[-1]
    count = out.shape[0]
    table = travelled[count:, :count].astype(jnp.float32)
    routes = table[0:1].astype(jnp.int32)
    gates = table[1:2] + table[2:3] + table[3:4]
    block_of = lax.rem(x_ref[0] + EXPERTS - routes, EXPERTS)
    placing = slots(block_of, block_of, count // EXPERTS).astype(jnp.bfloat16)
    rows = jnp.concatenate([block[...] for block in blocks], axis=0)
    picked = lax.dot_general(
        placing, rows, (((0,), (0,)), ((), ())), preferred_element_type=jnp.float32
    )
    mixed = travelled[:count, :].astype(jnp.float32) + as_column(gates) * picked
    out[...] = mixed.astype(jnp.bfloat16)


def combine(x_index, travelled, blocks):
    rows = travelled.shape[0] - EXTRA
    return call(
        combine_kernel,
        jax.ShapeDtypeStruct((rows, travelled.shape[1]), jnp.bfloat16),
        (x_index, travelled, *blocks),
        scalars=1,
        flops=2 * rows * travelled.size,
        moved=6 * travelled.size,
    )


def body(
    x_forward,
    x_backward,
    norm_gain,
    w_gate,
    w_up,
    w_down,
    routes_forward,
    routes_backward,
    gates_forward,
    gates_backward,
):
    weights = (w_gate[0], w_up[0], w_down[0])
    ring = lax.axis_size("z")
    far = ring // 2
    x_index = lax.axis_index("x").astype(jnp.int32).reshape(1)
    states = (x_forward[0], x_backward[0])
    routes = (routes_forward.reshape(1, -1), routes_backward.reshape(1, -1))
    gates = (gates_forward.reshape(1, -1), gates_backward.reshape(1, -1))
    travel = (1, -1)

    here, moved = [], []
    for m in range(2):
        buffer, travelling = prepare(states[m], routes[m], gates[m], norm_gain)
        here.append(lax.all_to_all(buffer, "x", split_axis=0, concat_axis=0, tiled=True))
        moved.append(shifted(travelling, "pipe", travel[m]))

    parts = [{}, {}]
    for m, part in enumerate(experts(here, *weights)):
        parts[m][0] = part
    moving = [{way: here[m] for way in (1, -1)} for m in range(2)]
    for step in range(1, far + 1):
        for m in range(2):
            arrived = []
            for way in (travel[m], -travel[m]):
                if step < far or way == travel[m]:
                    moving[m][way] = shifted(moving[m][way], "z", way)
                    arrived.append(way)
            results = experts(
                [moving[m][way] for way in arrived],
                *weights,
                after=(moved[m],) if step == 2 else (),
            )
            for way, part in zip(arrived, results):
                parts[m][-way * step] = part

    sums, last = [{}, {}], ()
    for stage in range(far):
        for m in range(2):
            left = {-travel[m]: far - stage, travel[m]: far - 1 - stage}
            ways = [way for way in left if left[way] > 0]
            totals = [parts[m][way * left[way]] for way in ways]
            if stage > 0:
                totals = add(totals, [sums[m][way] for way in ways], last)
                last = (totals[0],)
            for way, total in zip(ways, totals):
                sums[m][way] = shifted(total, "z", way)

    sections, columns = lax.axis_size("pipe"), lax.axis_size("x")
    done = []
    for m in range(2):
        blocks = split(x_index, parts[m][0], sums[m][1], sums[m][-1])
        returned = []
        for d, block in enumerate(blocks):
            pairs = [
                (s * columns + x, (s + travel[m]) % sections * columns + (x + d) % columns)
                for s in range(sections)
                for x in range(columns)
            ]
            returned.append(lax.ppermute(block, ("pipe", "x"), pairs))
        done.append(combine(x_index, moved[m], returned))
    return (done[0][None], done[1][None])


def solution(mesh):
    sections, members = mesh.devices.shape
    inner = Mesh(
        mesh.devices.reshape(sections, EXPERTS, members // EXPERTS), ("pipe", "x", "z")
    )
    tokens = P("pipe", ("x", "z"), None)
    placed = (
        tokens,
        tokens,
        P("pipe", None),
        P("pipe", None, ("x", "z")),
        P("pipe", None, ("x", "z")),
        tokens,
        tokens,
        tokens,
        tokens,
        tokens,
    )
    return jax.shard_map(
        body, mesh=inner, in_specs=placed, out_specs=(tokens, tokens), check_vma=False
    )
```

```python
import jax
import jax.numpy as jnp
from jax import lax
from jax.experimental import pallas as pl
from jax.experimental.pallas import tpu as pltpu
from jax.sharding import Mesh, PartitionSpec as P

EXPERTS = 4
EXTRA = 16
VMEM_BYTES = 48 * 1024 * 1024


def vmem_spec():
    return pl.BlockSpec(memory_space=pltpu.VMEM)


def call(kernel, out_shape, arguments, flops=0, moved=0, after=(), plain=0):
    specs = [pl.BlockSpec()] * plain + [vmem_spec()] * (len(arguments) - plain)
    specs += [pl.BlockSpec(memory_space=pl.ANY)] * len(after)
    used = len(arguments)

    def ordered(*refs):
        kernel(*refs[:used], *refs[used + len(after) :])

    return pl.pallas_call(
        ordered,
        out_shape=out_shape,
        in_specs=specs,
        out_specs=jax.tree.map(lambda _: vmem_spec(), out_shape),
        compiler_params=pltpu.CompilerParams(vmem_limit_bytes=VMEM_BYTES),
        cost_estimate=pl.CostEstimate(flops=flops, bytes_accessed=moved, transcendentals=0),
    )(*arguments, *after)


def shifted(array, axis, by):
    peers = lax.axis_size(axis)
    return lax.ppermute(array, axis, [(i, (i + by) % peers) for i in range(peers)])


def shifted_twice(array, along, across):
    peers, sections = lax.axis_size("z"), lax.axis_size("pipe")
    pairs = [
        (s * peers + z, (s + across) % sections * peers + (z + along) % peers)
        for s in range(sections)
        for z in range(peers)
    ]
    return lax.ppermute(array, ("pipe", "z"), pairs)


def as_column(row):
    count = row.shape[1]
    place = lax.broadcasted_iota(jnp.int32, (count, count), 0)
    other = lax.broadcasted_iota(jnp.int32, (count, count), 1)
    return jnp.sum(jnp.where(place == other, row, jnp.zeros_like(row)), axis=1, keepdims=True)


def slots(routes, blocks, per_block):
    count = routes.shape[1]
    place = lax.broadcasted_iota(jnp.int32, (count, count), 0)
    other = lax.broadcasted_iota(jnp.int32, (count, count), 1)
    earlier = (as_column(routes) == routes) & (place < other)
    rank = jnp.sum(earlier.astype(jnp.int32), axis=0, keepdims=True)
    return place == blocks * per_block + rank


def prepare_kernel(states, routes, gain, buffer):
    count = states.shape[0]
    values = states[...].astype(jnp.float32)
    mean_square = jnp.mean(values * values, axis=-1, keepdims=True)
    normed = (values * lax.rsqrt(mean_square + 1e-06) * gain[...]).astype(jnp.bfloat16)
    placing = slots(routes[...], routes[...], count // EXPERTS).astype(jnp.bfloat16)
    buffer[...] = jnp.dot(placing, normed, preferred_element_type=jnp.float32).astype(jnp.bfloat16)


def prepare(states, routes, gain, after):
    rows, width = states.shape
    return call(
        prepare_kernel,
        jax.ShapeDtypeStruct((rows, width), jnp.bfloat16),
        (states, routes, gain),
        flops=2 * rows * rows * width,
        moved=4 * rows * width,
        after=after,
        plain=3,
    )


def expert_kernel(blocks, gate_ref, up_ref, down_ref, *outs):
    width = gate_ref.shape[1]
    depth = gate_ref.shape[0]
    step = depth // 7
    rows = [ref[...] for ref in blocks]
    rows = rows[0] if len(rows) == 1 else jnp.concatenate(rows, axis=0)
    total = jnp.zeros((rows.shape[0], 2 * width), jnp.float32)
    for k in range(0, depth, step):
        both = jnp.concatenate([gate_ref[k : k + step, :], up_ref[k : k + step, :]], axis=1)
        total += jnp.dot(rows[:, k : k + step], both, preferred_element_type=jnp.float32)
    gate_part, up_part = total[:, :width], total[:, width:]
    hidden = (gate_part * jax.nn.sigmoid(gate_part) * up_part).astype(jnp.bfloat16)
    for k in range(0, depth, step):
        part = jnp.dot(hidden, down_ref[:, k : k + step], preferred_element_type=jnp.float32)
        part = part.astype(jnp.bfloat16)
        first = 0
        for out in outs:
            count = out.shape[0]
            out[:, k : k + step] = part[first : first + count]
            first += count


def experts(blocks, gate_cols, up_cols, down_rows, passed=0, after=()):
    number = len(blocks)

    def kernel(*refs):
        outs = refs[number + 3 :]
        expert_kernel(refs[:number], *refs[number : number + 3], *outs[:number])
        for block, out in zip(refs, outs[number:]):
            out[...] = block[...]

    row_count = sum(block.shape[0] for block in blocks)
    shapes = [jax.ShapeDtypeStruct(block.shape, jnp.bfloat16) for block in blocks]
    return call(
        kernel,
        tuple(shapes + shapes[:passed]),
        (*blocks, gate_cols, up_cols, down_rows),
        flops=6 * row_count * gate_cols.size,
        moved=6 * gate_cols.size + 4 * sum(block.size for block in blocks),
        after=after,
    )


def own_kernel(states, routes, gates, rows, gate_ref, up_ref, down_ref, out):
    count = states.shape[0]
    expert_kernel([rows], gate_ref, up_ref, down_ref, out.at[pl.ds(0, count)])
    out[count : 2 * count, :] = states[...]
    gate = gates[...]
    high = gate.astype(jnp.bfloat16).astype(jnp.float32)
    middle = (gate - high).astype(jnp.bfloat16).astype(jnp.float32)
    low = gate - high - middle
    row = lax.broadcasted_iota(jnp.int32, (EXTRA, count), 0)
    table = jnp.zeros((EXTRA, count), jnp.float32)
    for place, term in enumerate((routes[...].astype(jnp.float32), high, middle, low)):
        table = jnp.where(row == place, term, table)
    out[2 * count :, :] = jnp.zeros((EXTRA, states.shape[1]), jnp.bfloat16)
    out[2 * count :, :count] = table.astype(jnp.bfloat16)


def own_part(states, routes, gates, rows, gate_cols, up_cols, down_rows, after):
    count, width = states.shape
    return call(
        own_kernel,
        jax.ShapeDtypeStruct((2 * count + EXTRA, width), jnp.bfloat16),
        (states, routes, gates, rows, gate_cols, up_cols, down_rows),
        flops=6 * count * gate_cols.size,
        moved=6 * gate_cols.size + 10 * states.size,
        after=after,
        plain=3,
    )


def add(parts, sums, after):
    number = len(parts)

    def kernel(*refs):
        for part, received, out in zip(refs[:number], refs[number:], refs[2 * number :]):
            total = part[...].astype(jnp.float32) + received[...].astype(jnp.float32)
            out[...] = total.astype(jnp.bfloat16)

    return call(
        kernel,
        tuple(jax.ShapeDtypeStruct(part.shape, jnp.bfloat16) for part in parts),
        (*parts, *sums),
        flops=sum(part.size for part in parts),
        moved=6 * sum(part.size for part in parts),
        after=after,
    )


def finish_kernel(*refs):
    *refs, out = refs
    count = refs[1].shape[0]
    slot_count = count // EXPERTS
    number = len(refs) // 3
    for m in range(number):
        shipped, from_left, from_right = refs[3 * m : 3 * m + 3]
        total = shipped[:count, :].astype(jnp.float32) + from_left[...].astype(jnp.float32)
        total = (total + from_right[...].astype(jnp.float32)).astype(jnp.bfloat16)
        for e in range(EXPERTS):
            start = (e * number + m) * slot_count
            out[start : start + slot_count, :] = total[e * slot_count : (e + 1) * slot_count]


def finish(shipped, sums):
    rows, width = sums[0][1].shape
    arguments = []
    for m in range(2):
        arguments += [shipped[m], sums[m][1], sums[m][-1]]
    return call(
        finish_kernel,
        jax.ShapeDtypeStruct((2 * rows, width), jnp.bfloat16),
        arguments,
        flops=4 * rows * width,
        moved=16 * rows * width,
    )


def combine_kernel(*refs):
    *shipped, rows, out_forward, out_backward = refs
    for m, out in enumerate((out_forward, out_backward)):
        count = out.shape[0]
        slot_count = count // EXPERTS
        table = shipped[m][2 * count :, :count].astype(jnp.float32)
        routes = table[0:1].astype(jnp.int32)
        gates = table[1:2] + table[2:3] + table[3:4]
        placing = slots(routes, routes, slot_count).astype(jnp.bfloat16)
        starts = [(2 * e + m) * slot_count for e in range(EXPERTS)]
        returned = jnp.concatenate([rows[s : s + slot_count, :] for s in starts], axis=0)
        picked = lax.dot_general(
            placing, returned, (((0,), (0,)), ((), ())), preferred_element_type=jnp.float32
        )
        mixed = shipped[m][count : 2 * count, :].astype(jnp.float32) + as_column(gates) * picked
        out[...] = mixed.astype(jnp.bfloat16)


def combine(shipped, rows):
    count, width = rows.shape[0] // 2, rows.shape[1]
    return call(
        combine_kernel,
        (jax.ShapeDtypeStruct((count, width), jnp.bfloat16),) * 2,
        (*shipped, rows),
        flops=4 * count * count * width,
        moved=16 * count * width,
    )


def body(
    x_forward,
    x_backward,
    norm_gain,
    w_gate,
    w_up,
    w_down,
    routes_forward,
    routes_backward,
    gates_forward,
    gates_backward,
):
    weights = (w_gate[0], w_up[0], w_down[0])
    ring = lax.axis_size("z")
    far = ring // 2
    states = (x_forward[0], x_backward[0])
    routes = (routes_forward.reshape(1, -1), routes_backward.reshape(1, -1))
    gates = (gates_forward.reshape(1, -1), gates_backward.reshape(1, -1))
    travel = (1, -1)

    here, last = [], ()
    for m in range(2):
        buffer = prepare(states[m], routes[m], norm_gain, last)
        here.append(lax.all_to_all(buffer, "x", split_axis=0, concat_axis=0, tiled=True))
        last = (here[m],)

    parts = [{}, {}]
    moving = [{way: here[m] for way in (1, -1)} for m in range(2)]
    last, shipped = (), []
    for step in range(1, far + 1):
        for m in range(2):
            ways = [way for way in (travel[m], -travel[m]) if step < far or way == travel[m]]
            for way in ways:
                moving[m][way] = shifted(moving[m][way], "z", way)
        for m in range(2):
            ways = [way for way in (travel[m], -travel[m]) if step < far or way == travel[m]]
            if step == 1:
                own = own_part(states[m], routes[m], gates[m], here[m], *weights, last)
                shipped.append(shifted(own, "pipe", travel[m]))
                last = (own,)
            goes_on = [way for way in ways if step + 1 < far or (step < far and way == travel[m])]
            results = experts(
                [moving[m][way] for way in ways],
                *weights,
                passed=len(goes_on),
                after=last + ((shipped[m],) if step == far - 1 else ()),
            )
            last = (results[0],)
            for way, part in zip(ways, results):
                parts[m][-way * step] = part
            for way, block in zip(goes_on, results[len(ways) :]):
                moving[m][way] = block

    sums = [{}, {}]

    def send(m, stage, last):
        left = {-travel[m]: far - stage, travel[m]: far - 1 - stage}
        ways = [way for way in left if left[way] > 0]
        totals = [parts[m][way * left[way]] for way in ways]
        if stage > 0:
            totals = add(totals, [sums[m][way] for way in ways], last)
            last = (totals[0],)
        for way, total in zip(ways, totals):
            if left[way] == 1:
                sums[m][way] = shifted_twice(total, way, travel[m])
            else:
                sums[m][way] = shifted(total, "z", way)
        return last

    for stage in range(far):
        for m in range(2):
            last = send(m, stage, last)
    total = finish(shipped, sums)
    returned = lax.all_to_all(total, "x", split_axis=0, concat_axis=0, tiled=True)
    done_forward, done_backward = combine(shipped, returned)
    return (done_forward[None], done_backward[None])


def solution(mesh):
    sections, members = mesh.devices.shape
    inner = Mesh(
        mesh.devices.reshape(sections, EXPERTS, members // EXPERTS), ("pipe", "x", "z")
    )
    tokens = P("pipe", ("x", "z"), None)
    placed = (
        tokens,
        tokens,
        P("pipe", None),
        P("pipe", None, ("x", "z")),
        P("pipe", None, ("x", "z")),
        tokens,
        tokens,
        tokens,
        tokens,
        tokens,
    )
    return jax.shard_map(
        body, mesh=inner, in_specs=placed, out_specs=(tokens, tokens), check_vma=False
    )
```

```python
import functools

import jax
import jax.numpy as jnp
from jax import lax
from jax.experimental import pallas as pl
from jax.experimental.pallas import tpu as pltpu
from jax.sharding import Mesh, PartitionSpec as P

EXPERTS = 4
VMEM_BYTES = 48 * 1024 * 1024


def vmem_spec():
    return pl.BlockSpec(memory_space=pltpu.VMEM)


def call(kernel, out_shape, arguments, flops=0, moved=0, after=(), plain=0):
    specs = [pl.BlockSpec()] * plain + [vmem_spec()] * (len(arguments) - plain)
    specs += [pl.BlockSpec(memory_space=pl.ANY)] * len(after)
    used = len(arguments)

    def ordered(*refs):
        kernel(*refs[:used], *refs[used + len(after) :])

    return pl.pallas_call(
        ordered,
        out_shape=out_shape,
        in_specs=specs,
        out_specs=jax.tree.map(lambda _: vmem_spec(), out_shape),
        compiler_params=pltpu.CompilerParams(vmem_limit_bytes=VMEM_BYTES),
        cost_estimate=pl.CostEstimate(flops=flops, bytes_accessed=moved, transcendentals=0),
    )(*arguments, *after)


def shifted(array, axis, by):
    peers = lax.axis_size(axis)
    return lax.ppermute(array, axis, [(i, (i + by) % peers) for i in range(peers)])


def as_column(row):
    count = row.shape[1]
    place = lax.broadcasted_iota(jnp.int32, (count, count), 0)
    other = lax.broadcasted_iota(jnp.int32, (count, count), 1)
    return jnp.sum(jnp.where(place == other, row, jnp.zeros_like(row)), axis=1, keepdims=True)


def slots(routes, blocks, per_block):
    count = routes.shape[1]
    place = lax.broadcasted_iota(jnp.int32, (count, count), 0)
    other = lax.broadcasted_iota(jnp.int32, (count, count), 1)
    earlier = (as_column(routes) == routes) & (place < other)
    rank = jnp.sum(earlier.astype(jnp.int32), axis=0, keepdims=True)
    return place == blocks * per_block + rank


def prepare_kernel(states, routes, gain, buffer):
    count = states.shape[0]
    values = states[...].astype(jnp.float32)
    mean_square = jnp.mean(values * values, axis=-1, keepdims=True)
    normed = (values * lax.rsqrt(mean_square + 1e-06) * gain[...]).astype(jnp.bfloat16)
    placing = slots(routes[...], routes[...], count // EXPERTS).astype(jnp.bfloat16)
    buffer[...] = jnp.dot(placing, normed, preferred_element_type=jnp.float32).astype(jnp.bfloat16)


def prepare(states, routes, gain, after):
    rows, width = states.shape
    return call(
        prepare_kernel,
        jax.ShapeDtypeStruct((rows, width), jnp.bfloat16),
        (states, routes, gain),
        flops=2 * rows * rows * width,
        moved=4 * rows * width,
        after=after,
    )


def experts(blocks, gate_cols, up_cols, passed=0, after=()):
    number = len(blocks)
    width = gate_cols.shape[1]
    depth = gate_cols.shape[0]
    step = depth // 7

    def kernel(*refs):
        gate_ref, up_ref = refs[number : number + 2]
        outs = refs[number + 2 :]
        rows = [ref[...] for ref in refs[:number]]
        rows = rows[0] if number == 1 else jnp.concatenate(rows, axis=0)
        total = jnp.zeros((rows.shape[0], 2 * width), jnp.float32)
        for k in range(0, depth, step):
            both = jnp.concatenate([gate_ref[k : k + step, :], up_ref[k : k + step, :]], axis=1)
            total += jnp.dot(rows[:, k : k + step], both, preferred_element_type=jnp.float32)
        gate_part, up_part = total[:, :width], total[:, width:]
        hidden = (gate_part * jax.nn.sigmoid(gate_part) * up_part).astype(jnp.bfloat16)
        first = 0
        for out in outs[:number]:
            out[...] = hidden[first : first + out.shape[0]]
            first += out.shape[0]
        for block, out in zip(refs, outs[number:]):
            out[...] = block[...]

    row_count = sum(block.shape[0] for block in blocks)
    shapes = [jax.ShapeDtypeStruct((block.shape[0], width), jnp.bfloat16) for block in blocks]
    shapes += [jax.ShapeDtypeStruct(block.shape, jnp.bfloat16) for block in blocks[:passed]]
    return call(
        kernel,
        tuple(shapes),
        (*blocks, gate_cols, up_cols),
        flops=4 * row_count * gate_cols.size,
        moved=4 * gate_cols.size + 4 * sum(block.size for block in blocks),
        after=after,
    )


def down(hiddens, rows_of, kind, after=()):
    number = len(hiddens)
    count = hiddens[0][0].shape[0]
    width = rows_of[0].shape[1]
    step = width // 7

    def kernel(*refs):
        *refs, out = refs
        left = [ref[first : first + count, :] for ref, (_, first) in zip(refs, hiddens)]
        left = left[0] if number == 1 else jnp.concatenate(left, axis=1)
        for k in range(0, width, step):
            right = [ref[:, k : k + step] for ref in refs[number:]]
            right = right[0] if number == 1 else jnp.concatenate(right, axis=0)
            part = jnp.dot(left, right, preferred_element_type=jnp.float32)
            out[:, k : k + step] = part.astype(kind)

    return call(
        kernel,
        jax.ShapeDtypeStruct((count, width), kind),
        (*[hidden for hidden, _ in hiddens], *rows_of),
        flops=2 * number * count * rows_of[0].size,
        moved=2 * number * rows_of[0].size + 4 * count * width,
        after=after,
    )


def finish_kernel(*refs):
    *refs, out = refs
    count = refs[0].shape[0]
    slot_count = count // EXPERTS
    for m in range(2):
        own, from_left, from_right = refs[3 * m : 3 * m + 3]
        total = own[...].astype(jnp.float32) + from_left[...].astype(jnp.float32)
        total = (total + from_right[...].astype(jnp.float32)).astype(jnp.bfloat16)
        for e in range(EXPERTS):
            start = (2 * e + m) * slot_count
            out[start : start + slot_count, :] = total[e * slot_count : (e + 1) * slot_count]


def finish(own, sums):
    rows, width = own[0].shape
    arguments = []
    for m in range(2):
        arguments += [own[m], sums[m][1], sums[m][-1]]
    return call(
        finish_kernel,
        jax.ShapeDtypeStruct((2 * rows, width), jnp.bfloat16),
        arguments,
        flops=4 * rows * width,
        moved=16 * rows * width,
    )


def combine_kernel(m, states, routes, gates, rows, out):
    count = out.shape[0]
    slot_count = count // EXPERTS
    placing = slots(routes[...], routes[...], slot_count).astype(jnp.bfloat16)
    starts = [(2 * e + m) * slot_count for e in range(EXPERTS)]
    returned = jnp.concatenate([rows[s : s + slot_count, :] for s in starts], axis=0)
    picked = lax.dot_general(
        placing, returned, (((0,), (0,)), ((), ())), preferred_element_type=jnp.float32
    )
    mixed = states[...].astype(jnp.float32) + as_column(gates[...]) * picked
    out[...] = mixed.astype(jnp.bfloat16)


def combine(m, states, routes, gates, rows, after):
    return call(
        functools.partial(combine_kernel, m),
        jax.ShapeDtypeStruct(states.shape, jnp.bfloat16),
        (states, routes, gates, rows),
        flops=2 * states.shape[0] * states.size,
        moved=8 * states.size,
        after=after,
    )


def body(
    x_forward,
    x_backward,
    norm_gain,
    w_gate,
    w_up,
    w_down,
    routes_forward,
    routes_backward,
    gates_forward,
    gates_backward,
):
    weights = (w_gate[0], w_up[0])
    down_here = w_down[0]
    ring = lax.axis_size("z")
    far = ring // 2
    states = (x_forward[0], x_backward[0])
    routes = (routes_forward.reshape(1, -1), routes_backward.reshape(1, -1))
    gates = (gates_forward.reshape(1, -1), gates_backward.reshape(1, -1))
    travel = (1, -1)

    here, last = [], ()
    for m in range(2):
        buffer = prepare(states[m], routes[m], norm_gain, last)
        here.append(lax.all_to_all(buffer, "x", split_axis=0, concat_axis=0, tiled=True))
        last = (here[m],)

    down_from = {way: shifted(down_here, "z", way) for way in (1, -1)}

    hidden = [{}, {}]
    own = experts(here, *weights, after=(down_from[1], down_from[-1]))
    last = (own[0],)
    for m in range(2):
        hidden[m][0] = own[m]
    moving = [{way: here[m] for way in (1, -1)} for m in range(2)]
    for step in range(1, far + 1):
        for m in range(2):
            ways = [way for way in (travel[m], -travel[m]) if step < far or way == travel[m]]
            for way in ways:
                moving[m][way] = shifted(moving[m][way], "z", way)
            goes_on = [way for way in ways if step + 1 < far or (step < far and way == travel[m])]
            results = experts(
                [moving[m][way] for way in ways], *weights, passed=len(goes_on), after=last
            )
            last = (results[0],)
            for way, part in zip(ways, results):
                hidden[m][-way * step] = part
            for way, block in zip(goes_on, results[len(ways) :]):
                moving[m][way] = block

    count = here[0].shape[0]
    ahead, behind = [], []
    for m, t in enumerate(travel):
        ahead.append(
            shifted(
                jnp.concatenate([hidden[m][k * t] for k in (3, -2, 1)], axis=0), "z", t
            )
        )
    for m, t in enumerate(travel):
        behind.append(
            shifted(jnp.concatenate([hidden[m][k * t] for k in (-4, -1)], axis=0), "z", -t)
        )
    sums = [{}, {}]
    for m, t in enumerate(travel):
        part = down(
            [(hidden[m][2 * t], 0), (ahead[m], 0)], [down_here, down_from[t]], jnp.bfloat16, last
        )
        last = (part,)
        sums[m][1] = shifted(part, "z", 2 * t)
    rows_of = [(down_here, down_from[t], down_from[-t]) for t in travel]
    for m, t in enumerate(travel):
        parts = [(hidden[m][-3 * t], 0), (ahead[m], count), (behind[m], 0)]
        part = down(parts, rows_of[m], jnp.bfloat16, last)
        last = (part,)
        sums[m][-1] = shifted(part, "z", -3 * t)
    own = []
    for m, t in enumerate(travel):
        parts = [(hidden[m][0], 0), (ahead[m], 2 * count), (behind[m], count)]
        own.append(down(parts, rows_of[m], jnp.float32, last))
        last = (own[m],)

    total = finish(own, sums)
    returned = lax.all_to_all(total, "x", split_axis=0, concat_axis=0, tiled=True)
    done, last = [], ()
    for m in range(2):
        result = combine(m, states[m], routes[m], gates[m], returned, last)
        done.append(shifted(result, "pipe", travel[m])[None])
        last = (result,)
    return (done[0], done[1])


def solution(mesh):
    sections, members = mesh.devices.shape
    inner = Mesh(
        mesh.devices.reshape(sections, EXPERTS, members // EXPERTS), ("pipe", "x", "z")
    )
    tokens = P("pipe", ("x", "z"), None)
    placed = (
        tokens,
        tokens,
        P("pipe", None),
        P("pipe", None, ("x", "z")),
        P("pipe", None, ("x", "z")),
        tokens,
        tokens,
        tokens,
        tokens,
        tokens,
    )
    return jax.shard_map(
        body, mesh=inner, in_specs=placed, out_specs=(tokens, tokens), check_vma=False
    )
```

```python
import functools

import jax
import jax.numpy as jnp
from jax import lax
from jax.experimental import pallas as pl
from jax.experimental.pallas import tpu as pltpu
from jax.sharding import Mesh, PartitionSpec as P

EXPERTS = 4
VMEM_BYTES = 48 * 1024 * 1024


def vmem_spec():
    return pl.BlockSpec(memory_space=pltpu.VMEM)


def call(kernel, out_shape, arguments, flops=0, moved=0, after=(), plain=0):
    specs = [pl.BlockSpec()] * plain + [vmem_spec()] * (len(arguments) - plain)
    specs += [pl.BlockSpec(memory_space=pl.ANY)] * len(after)
    used = len(arguments)

    def ordered(*refs):
        kernel(*refs[:used], *refs[used + len(after) :])

    return pl.pallas_call(
        ordered,
        out_shape=out_shape,
        in_specs=specs,
        out_specs=jax.tree.map(lambda _: vmem_spec(), out_shape),
        compiler_params=pltpu.CompilerParams(vmem_limit_bytes=VMEM_BYTES),
        cost_estimate=pl.CostEstimate(flops=flops, bytes_accessed=moved, transcendentals=0),
    )(*arguments, *after)


def shifted(array, axis, by):
    peers = lax.axis_size(axis)
    return lax.ppermute(array, axis, [(i, (i + by) % peers) for i in range(peers)])


def as_column(row):
    count = row.shape[1]
    place = lax.broadcasted_iota(jnp.int32, (count, count), 0)
    other = lax.broadcasted_iota(jnp.int32, (count, count), 1)
    return jnp.sum(jnp.where(place == other, row, jnp.zeros_like(row)), axis=1, keepdims=True)


def slots(routes, blocks, per_block):
    count = routes.shape[1]
    place = lax.broadcasted_iota(jnp.int32, (count, count), 0)
    other = lax.broadcasted_iota(jnp.int32, (count, count), 1)
    earlier = (as_column(routes) == routes) & (place < other)
    rank = jnp.sum(earlier.astype(jnp.int32), axis=0, keepdims=True)
    return place == blocks * per_block + rank


def prepare_kernel(*refs):
    sources, (buffer, *held), arrived = refs[:5], refs[5:11], refs[11]
    copies = [
        pltpu.make_async_copy(source, place, arrived.at[i])
        for i, (source, place) in enumerate(zip(sources, held))
    ]
    for copy in copies:
        copy.start()
    for copy in copies:
        copy.wait()
    gain, *pairs = held
    count = pairs[0].shape[0]
    slot_count = count // EXPERTS
    for m in range(2):
        states, routes = pairs[m], pairs[2 + m]
        values = states[...].astype(jnp.float32)
        mean_square = jnp.mean(values * values, axis=-1, keepdims=True)
        normed = (values * lax.rsqrt(mean_square + 1e-06) * gain[...]).astype(jnp.bfloat16)
        placing = slots(routes[...], routes[...], slot_count).astype(jnp.bfloat16)
        placed = jnp.dot(placing, normed, preferred_element_type=jnp.float32)
        placed = placed.astype(jnp.bfloat16)
        for e in range(EXPERTS):
            start = (e * 2 + m) * slot_count
            buffer[start : start + slot_count, :] = placed[e * slot_count : (e + 1) * slot_count]


def prepare(states, routes, gain):
    rows, width = states[0].shape
    arguments = (gain, *states, *routes)
    return pl.pallas_call(
        prepare_kernel,
        out_shape=jax.ShapeDtypeStruct((2 * rows, width), jnp.bfloat16),
        in_specs=[pl.BlockSpec(memory_space=pl.ANY)] * 5,
        out_specs=vmem_spec(),
        scratch_shapes=[pltpu.VMEM(array.shape, array.dtype) for array in arguments]
        + [pltpu.SemaphoreType.DMA((5,))],
        compiler_params=pltpu.CompilerParams(vmem_limit_bytes=VMEM_BYTES),
        cost_estimate=pl.CostEstimate(
            flops=4 * rows * rows * width, bytes_accessed=8 * rows * width, transcendentals=0
        ),
    )(*arguments)


def parted_kernel(gathered, *outs):
    slot_count = outs[0].shape[0] // EXPERTS
    for m, out in enumerate(outs):
        for e in range(EXPERTS):
            start = (2 * e + m) * slot_count
            out[e * slot_count : (e + 1) * slot_count, :] = gathered[start : start + slot_count, :]


def parted(gathered, after):
    rows, width = gathered.shape
    return call(
        parted_kernel,
        (jax.ShapeDtypeStruct((rows // 2, width), jnp.bfloat16),) * 2,
        (gathered,),
        moved=4 * gathered.size,
        after=after,
    )


def experts(blocks, gate_cols, up_cols, passed=0, after=()):
    number = len(blocks)
    width = gate_cols.shape[1]
    depth = gate_cols.shape[0]
    step = depth // 7

    def kernel(*refs):
        gate_ref, up_ref = refs[number : number + 2]
        outs = refs[number + 2 :]
        rows = [ref[...] for ref in refs[:number]]
        rows = rows[0] if number == 1 else jnp.concatenate(rows, axis=0)
        total = jnp.zeros((rows.shape[0], 2 * width), jnp.float32)
        for k in range(0, depth, step):
            both = jnp.concatenate([gate_ref[k : k + step, :], up_ref[k : k + step, :]], axis=1)
            total += jnp.dot(rows[:, k : k + step], both, preferred_element_type=jnp.float32)
        gate_part, up_part = total[:, :width], total[:, width:]
        hidden = (gate_part * jax.nn.sigmoid(gate_part) * up_part).astype(jnp.bfloat16)
        first = 0
        for out in outs[:number]:
            out[...] = hidden[first : first + out.shape[0]]
            first += out.shape[0]
        for block, out in zip(refs, outs[number:]):
            out[...] = block[...]

    row_count = sum(block.shape[0] for block in blocks)
    shapes = [jax.ShapeDtypeStruct((block.shape[0], width), jnp.bfloat16) for block in blocks]
    shapes += [jax.ShapeDtypeStruct(block.shape, jnp.bfloat16) for block in blocks[:passed]]
    return call(
        kernel,
        tuple(shapes),
        (*blocks, gate_cols, up_cols),
        flops=4 * row_count * gate_cols.size,
        moved=4 * gate_cols.size + 4 * sum(block.size for block in blocks),
        after=after,
    )


def down(hiddens, rows_of, kind, after=()):
    number = len(hiddens)
    count = hiddens[0][0].shape[0]
    width = rows_of[0].shape[1]
    step = width // 7

    def kernel(*refs):
        *refs, out = refs
        left = [ref[first : first + count, :] for ref, (_, first) in zip(refs, hiddens)]
        left = left[0] if number == 1 else jnp.concatenate(left, axis=1)
        for k in range(0, width, step):
            right = [ref[:, k : k + step] for ref in refs[number:]]
            right = right[0] if number == 1 else jnp.concatenate(right, axis=0)
            part = jnp.dot(left, right, preferred_element_type=jnp.float32)
            out[:, k : k + step] = part.astype(kind)

    return call(
        kernel,
        jax.ShapeDtypeStruct((count, width), kind),
        (*[hidden for hidden, _ in hiddens], *rows_of),
        flops=2 * number * count * rows_of[0].size,
        moved=2 * number * rows_of[0].size + 4 * count * width,
        after=after,
    )


def finish_kernel(*refs):
    *refs, out = refs
    count = refs[0].shape[0]
    slot_count = count // EXPERTS
    for m in range(2):
        own, from_left, from_right = refs[3 * m : 3 * m + 3]
        total = own[...].astype(jnp.float32) + from_left[...].astype(jnp.float32)
        total = (total + from_right[...].astype(jnp.float32)).astype(jnp.bfloat16)
        for e in range(EXPERTS):
            start = (2 * e + m) * slot_count
            out[start : start + slot_count, :] = total[e * slot_count : (e + 1) * slot_count]


def finish(own, sums):
    rows, width = own[0].shape
    arguments = []
    for m in range(2):
        arguments += [own[m], sums[m][1], sums[m][-1]]
    return call(
        finish_kernel,
        jax.ShapeDtypeStruct((2 * rows, width), jnp.bfloat16),
        arguments,
        flops=4 * rows * width,
        moved=16 * rows * width,
    )


def combine_kernel(m, states, routes, gates, rows, out):
    count = out.shape[0]
    slot_count = count // EXPERTS
    placing = slots(routes[...], routes[...], slot_count).astype(jnp.bfloat16)
    starts = [(2 * e + m) * slot_count for e in range(EXPERTS)]
    returned = jnp.concatenate([rows[s : s + slot_count, :] for s in starts], axis=0)
    picked = lax.dot_general(
        placing, returned, (((0,), (0,)), ((), ())), preferred_element_type=jnp.float32
    )
    mixed = states[...].astype(jnp.float32) + as_column(gates[...]) * picked
    out[...] = mixed.astype(jnp.bfloat16)


def combine(m, states, routes, gates, rows, after):
    return call(
        functools.partial(combine_kernel, m),
        jax.ShapeDtypeStruct(states.shape, jnp.bfloat16),
        (states, routes, gates, rows),
        flops=2 * states.shape[0] * states.size,
        moved=8 * states.size,
        after=after,
    )


def body(
    x_forward,
    x_backward,
    norm_gain,
    w_gate,
    w_up,
    w_down,
    routes_forward,
    routes_backward,
    gates_forward,
    gates_backward,
):
    weights = (w_gate[0], w_up[0])
    down_here = w_down[0]
    ring = lax.axis_size("z")
    far = ring // 2
    states = (x_forward[0], x_backward[0])
    routes = (routes_forward.reshape(1, -1), routes_backward.reshape(1, -1))
    gates = (gates_forward.reshape(1, -1), gates_backward.reshape(1, -1))
    travel = (1, -1)

    down_from = {way: shifted(down_here, "z", way) for way in (1, -1)}

    gathered = lax.all_to_all(
        prepare(states, routes, norm_gain), "x", split_axis=0, concat_axis=0, tiled=True
    )
    here = parted(gathered, (down_from[1], down_from[-1]))

    hidden = [{}, {}]
    own = experts(here, *weights, after=(down_from[1], down_from[-1]))
    last = (own[0],)
    for m in range(2):
        hidden[m][0] = own[m]
    moving = [{way: here[m] for way in (1, -1)} for m in range(2)]
    for step in range(1, far + 1):
        for m in range(2):
            ways = [way for way in (travel[m], -travel[m]) if step < far or way == travel[m]]
            for way in ways:
                moving[m][way] = shifted(moving[m][way], "z", way)
            goes_on = [way for way in ways if step + 1 < far or (step < far and way == travel[m])]
            results = experts(
                [moving[m][way] for way in ways], *weights, passed=len(goes_on), after=last
            )
            last = (results[0],)
            for way, part in zip(ways, results):
                hidden[m][-way * step] = part
            for way, block in zip(goes_on, results[len(ways) :]):
                moving[m][way] = block

    count = here[0].shape[0]
    ahead, behind = [], []
    for m, t in enumerate(travel):
        ahead.append(
            shifted(
                jnp.concatenate([hidden[m][k * t] for k in (3, -2, 1)], axis=0), "z", t
            )
        )
    for m, t in enumerate(travel):
        behind.append(
            shifted(jnp.concatenate([hidden[m][k * t] for k in (-4, -1)], axis=0), "z", -t)
        )
    sums = [{}, {}]
    for m, t in enumerate(travel):
        part = down(
            [(hidden[m][2 * t], 0), (ahead[m], 0)], [down_here, down_from[t]], jnp.bfloat16, last
        )
        last = (part,)
        sums[m][1] = shifted(part, "z", 2 * t)
    rows_of = [(down_here, down_from[t], down_from[-t]) for t in travel]
    for m, t in enumerate(travel):
        parts = [(hidden[m][-3 * t], 0), (ahead[m], count), (behind[m], 0)]
        part = down(parts, rows_of[m], jnp.bfloat16, last)
        last = (part,)
        sums[m][-1] = shifted(part, "z", -3 * t)
    own = []
    for m, t in enumerate(travel):
        parts = [(hidden[m][0], 0), (ahead[m], 2 * count), (behind[m], count)]
        own.append(down(parts, rows_of[m], jnp.float32, last))
        last = (own[m],)

    total = finish(own, sums)
    returned = lax.all_to_all(total, "x", split_axis=0, concat_axis=0, tiled=True)
    done, last = [], ()
    for m in range(2):
        result = combine(m, states[m], routes[m], gates[m], returned, last)
        done.append(shifted(result, "pipe", travel[m])[None])
        last = (result,)
    return (done[0], done[1])


def solution(mesh):
    sections, members = mesh.devices.shape
    inner = Mesh(
        mesh.devices.reshape(sections, EXPERTS, members // EXPERTS), ("pipe", "x", "z")
    )
    tokens = P("pipe", ("x", "z"), None)
    placed = (
        tokens,
        tokens,
        P("pipe", None),
        P("pipe", None, ("x", "z")),
        P("pipe", None, ("x", "z")),
        tokens,
        tokens,
        tokens,
        tokens,
        tokens,
    )
    return jax.shard_map(
        body, mesh=inner, in_specs=placed, out_specs=(tokens, tokens), check_vma=False
    )
```

```python
import jax
import jax.numpy as jnp
from jax import lax
from jax.experimental import pallas as pl
from jax.experimental.pallas import tpu as pltpu
from jax.sharding import Mesh, PartitionSpec as P

EXPERTS = 4
VMEM_BYTES = 48 * 1024 * 1024


def vmem_spec():
    return pl.BlockSpec(memory_space=pltpu.VMEM)


def call(kernel, out_shape, arguments, flops=0, moved=0, after=(), plain=0):
    specs = [pl.BlockSpec()] * plain + [vmem_spec()] * (len(arguments) - plain)
    specs += [pl.BlockSpec(memory_space=pl.ANY)] * len(after)
    used = len(arguments)

    def ordered(*refs):
        kernel(*refs[:used], *refs[used + len(after) :])

    return pl.pallas_call(
        ordered,
        out_shape=out_shape,
        in_specs=specs,
        out_specs=jax.tree.map(lambda _: vmem_spec(), out_shape),
        compiler_params=pltpu.CompilerParams(vmem_limit_bytes=VMEM_BYTES),
        cost_estimate=pl.CostEstimate(flops=flops, bytes_accessed=moved, transcendentals=0),
    )(*arguments, *after)


def shifted(array, axis, by):
    peers = lax.axis_size(axis)
    return lax.ppermute(array, axis, [(i, (i + by) % peers) for i in range(peers)])


def as_column(row):
    count = row.shape[1]
    place = lax.broadcasted_iota(jnp.int32, (count, count), 0)
    other = lax.broadcasted_iota(jnp.int32, (count, count), 1)
    return jnp.sum(jnp.where(place == other, row, jnp.zeros_like(row)), axis=1, keepdims=True)


def slots(routes, blocks, per_block):
    count = routes.shape[1]
    place = lax.broadcasted_iota(jnp.int32, (count, count), 0)
    other = lax.broadcasted_iota(jnp.int32, (count, count), 1)
    earlier = (as_column(routes) == routes) & (place < other)
    rank = jnp.sum(earlier.astype(jnp.int32), axis=0, keepdims=True)
    return place == blocks * per_block + rank


def prepare_kernel(*refs):
    sources, (buffer, *held), arrived = refs[:5], refs[5:11], refs[11]
    copies = [
        pltpu.make_async_copy(source, place, arrived.at[i])
        for i, (source, place) in enumerate(zip(sources, held))
    ]
    for copy in copies:
        copy.start()
    for copy in copies:
        copy.wait()
    gain, *pairs = held
    count = pairs[0].shape[0]
    slot_count = count // EXPERTS
    for m in range(2):
        states, routes = pairs[m], pairs[2 + m]
        values = states[...].astype(jnp.float32)
        mean_square = jnp.mean(values * values, axis=-1, keepdims=True)
        normed = (values * lax.rsqrt(mean_square + 1e-06) * gain[...]).astype(jnp.bfloat16)
        placing = slots(routes[...], routes[...], slot_count).astype(jnp.bfloat16)
        placed = jnp.dot(placing, normed, preferred_element_type=jnp.float32)
        placed = placed.astype(jnp.bfloat16)
        for e in range(EXPERTS):
            start = (e * 2 + m) * slot_count
            buffer[start : start + slot_count, :] = placed[e * slot_count : (e + 1) * slot_count]


def prepare(states, routes, gain):
    rows, width = states[0].shape
    arguments = (gain, *states, *routes)
    return pl.pallas_call(
        prepare_kernel,
        out_shape=jax.ShapeDtypeStruct((2 * rows, width), jnp.bfloat16),
        in_specs=[pl.BlockSpec(memory_space=pl.ANY)] * 5,
        out_specs=vmem_spec(),
        scratch_shapes=[pltpu.VMEM(array.shape, array.dtype) for array in arguments]
        + [pltpu.SemaphoreType.DMA((5,))],
        compiler_params=pltpu.CompilerParams(vmem_limit_bytes=VMEM_BYTES),
        cost_estimate=pl.CostEstimate(
            flops=4 * rows * rows * width, bytes_accessed=8 * rows * width, transcendentals=0
        ),
    )(*arguments)


def parted_kernel(gathered, *outs):
    slot_count = outs[0].shape[0] // EXPERTS
    for m, out in enumerate(outs):
        for e in range(EXPERTS):
            start = (2 * e + m) * slot_count
            out[e * slot_count : (e + 1) * slot_count, :] = gathered[start : start + slot_count, :]


def parted(gathered, after):
    rows, width = gathered.shape
    return call(
        parted_kernel,
        (jax.ShapeDtypeStruct((rows // 2, width), jnp.bfloat16),) * 2,
        (gathered,),
        moved=4 * gathered.size,
        after=after,
    )


def experts(blocks, gate_cols, up_cols, passed=0, after=()):
    number = len(blocks)
    width = gate_cols.shape[1]
    depth = gate_cols.shape[0]
    step = depth // 7

    def kernel(*refs):
        gate_ref, up_ref = refs[number : number + 2]
        outs = refs[number + 2 :]
        rows = [ref[...] for ref in refs[:number]]
        rows = rows[0] if number == 1 else jnp.concatenate(rows, axis=0)
        total = jnp.zeros((rows.shape[0], 2 * width), jnp.float32)
        for k in range(0, depth, step):
            both = jnp.concatenate([gate_ref[k : k + step, :], up_ref[k : k + step, :]], axis=1)
            total += jnp.dot(rows[:, k : k + step], both, preferred_element_type=jnp.float32)
        gate_part, up_part = total[:, :width], total[:, width:]
        hidden = (gate_part * jax.nn.sigmoid(gate_part) * up_part).astype(jnp.bfloat16)
        first = 0
        for out in outs[:number]:
            out[...] = hidden[first : first + out.shape[0]]
            first += out.shape[0]
        for block, out in zip(refs, outs[number:]):
            out[...] = block[...]

    row_count = sum(block.shape[0] for block in blocks)
    shapes = [jax.ShapeDtypeStruct((block.shape[0], width), jnp.bfloat16) for block in blocks]
    shapes += [jax.ShapeDtypeStruct(block.shape, jnp.bfloat16) for block in blocks[:passed]]
    return call(
        kernel,
        tuple(shapes),
        (*blocks, gate_cols, up_cols),
        flops=4 * row_count * gate_cols.size,
        moved=4 * gate_cols.size + 4 * sum(block.size for block in blocks),
        after=after,
    )


def down(hiddens, rows_of, kind, after=()):
    number = len(hiddens)
    count = hiddens[0][0].shape[0]
    width = rows_of[0].shape[1]
    step = width // 7

    def kernel(*refs):
        *refs, out = refs
        left = [ref[first : first + count, :] for ref, (_, first) in zip(refs, hiddens)]
        left = left[0] if number == 1 else jnp.concatenate(left, axis=1)
        for k in range(0, width, step):
            right = [ref[:, k : k + step] for ref in refs[number:]]
            right = right[0] if number == 1 else jnp.concatenate(right, axis=0)
            part = jnp.dot(left, right, preferred_element_type=jnp.float32)
            out[:, k : k + step] = part.astype(kind)

    return call(
        kernel,
        jax.ShapeDtypeStruct((count, width), kind),
        (*[hidden for hidden, _ in hiddens], *rows_of),
        flops=2 * number * count * rows_of[0].size,
        moved=2 * number * rows_of[0].size + 4 * count * width,
        after=after,
    )


def finish_kernel(*refs):
    *refs, out = refs
    count = refs[0].shape[0]
    slot_count = count // EXPERTS
    for m in range(2):
        own, from_left, from_right = refs[3 * m : 3 * m + 3]
        total = own[...].astype(jnp.float32) + from_left[...].astype(jnp.float32)
        total = (total + from_right[...].astype(jnp.float32)).astype(jnp.bfloat16)
        for e in range(EXPERTS):
            start = (2 * e + m) * slot_count
            out[start : start + slot_count, :] = total[e * slot_count : (e + 1) * slot_count]


def finish(own, sums):
    rows, width = own[0].shape
    arguments = []
    for m in range(2):
        arguments += [own[m], sums[m][1], sums[m][-1]]
    return call(
        finish_kernel,
        jax.ShapeDtypeStruct((2 * rows, width), jnp.bfloat16),
        arguments,
        flops=4 * rows * width,
        moved=16 * rows * width,
    )


def combine_kernel(*refs):
    rows, *outs = refs[6:]
    for m, out in enumerate(outs):
        states, routes, gates = refs[m], refs[2 + m], refs[4 + m]
        count = out.shape[0]
        slot_count = count // EXPERTS
        placing = slots(routes[...], routes[...], slot_count).astype(jnp.bfloat16)
        starts = [(2 * e + m) * slot_count for e in range(EXPERTS)]
        returned = jnp.concatenate([rows[s : s + slot_count, :] for s in starts], axis=0)
        picked = lax.dot_general(
            placing, returned, (((0,), (0,)), ((), ())), preferred_element_type=jnp.float32
        )
        mixed = states[...].astype(jnp.float32) + as_column(gates[...]) * picked
        out[...] = mixed.astype(jnp.bfloat16)


def combine(states, routes, gates, rows):
    return call(
        combine_kernel,
        tuple(jax.ShapeDtypeStruct(array.shape, jnp.bfloat16) for array in states),
        (*states, *routes, *gates, rows),
        flops=4 * states[0].shape[0] * states[0].size,
        moved=16 * states[0].size,
    )


def body(
    x_forward,
    x_backward,
    norm_gain,
    w_gate,
    w_up,
    w_down,
    routes_forward,
    routes_backward,
    gates_forward,
    gates_backward,
):
    weights = (w_gate[0], w_up[0])
    down_here = w_down[0]
    ring = lax.axis_size("z")
    far = ring // 2
    states = (x_forward[0], x_backward[0])
    routes = (routes_forward.reshape(1, -1), routes_backward.reshape(1, -1))
    gates = (gates_forward.reshape(1, -1), gates_backward.reshape(1, -1))
    travel = (1, -1)

    down_from = {way: shifted(down_here, "z", way) for way in (1, -1)}

    gathered = lax.all_to_all(
        prepare(states, routes, norm_gain), "x", split_axis=0, concat_axis=0, tiled=True
    )
    here = parted(gathered, (down_from[1], down_from[-1]))

    hidden = [{}, {}]
    own = experts(here, *weights, after=(down_from[1], down_from[-1]))
    last = (own[0],)
    for m in range(2):
        hidden[m][0] = own[m]
    moving = [{way: here[m] for way in (1, -1)} for m in range(2)]
    for step in range(1, far + 1):
        for m in range(2):
            ways = [way for way in (travel[m], -travel[m]) if step < far or way == travel[m]]
            for way in ways:
                moving[m][way] = shifted(moving[m][way], "z", way)
            goes_on = [way for way in ways if step + 1 < far or (step < far and way == travel[m])]
            results = experts(
                [moving[m][way] for way in ways], *weights, passed=len(goes_on), after=last
            )
            last = (results[0],)
            for way, part in zip(ways, results):
                hidden[m][-way * step] = part
            for way, block in zip(goes_on, results[len(ways) :]):
                moving[m][way] = block

    count = here[0].shape[0]
    ahead, behind = [], []
    for m, t in enumerate(travel):
        ahead.append(
            shifted(
                jnp.concatenate([hidden[m][k * t] for k in (3, -2, 1)], axis=0), "z", t
            )
        )
    for m, t in enumerate(travel):
        behind.append(
            shifted(jnp.concatenate([hidden[m][k * t] for k in (-4, -1)], axis=0), "z", -t)
        )
    sums = [{}, {}]
    for m, t in enumerate(travel):
        part = down(
            [(hidden[m][2 * t], 0), (ahead[m], 0)], [down_here, down_from[t]], jnp.bfloat16, last
        )
        last = (part,)
        sums[m][1] = shifted(part, "z", 2 * t)
    rows_of = [(down_here, down_from[t], down_from[-t]) for t in travel]
    for m, t in enumerate(travel):
        parts = [(hidden[m][-3 * t], 0), (ahead[m], count), (behind[m], 0)]
        part = down(parts, rows_of[m], jnp.bfloat16, last)
        last = (part,)
        sums[m][-1] = shifted(part, "z", -3 * t)
    own = []
    for m, t in enumerate(travel):
        parts = [(hidden[m][0], 0), (ahead[m], 2 * count), (behind[m], count)]
        own.append(down(parts, rows_of[m], jnp.float32, last))
        last = (own[m],)

    total = finish(own, sums)
    returned = lax.all_to_all(total, "x", split_axis=0, concat_axis=0, tiled=True)
    results = combine(states, routes, gates, returned)
    done = [shifted(result, "pipe", t)[None] for result, t in zip(results, travel)]
    return (done[0], done[1])


def solution(mesh):
    sections, members = mesh.devices.shape
    inner = Mesh(
        mesh.devices.reshape(sections, EXPERTS, members // EXPERTS), ("pipe", "x", "z")
    )
    tokens = P("pipe", ("x", "z"), None)
    placed = (
        tokens,
        tokens,
        P("pipe", None),
        P("pipe", None, ("x", "z")),
        P("pipe", None, ("x", "z")),
        tokens,
        tokens,
        tokens,
        tokens,
        tokens,
    )
    return jax.shard_map(
        body, mesh=inner, in_specs=placed, out_specs=(tokens, tokens), check_vma=False
    )
```
